768 devices in a mesh: diag: 32 (over x_lo, y, core), off: 24 (over x_hi, z).
Axes of the slice: x: 4 (x_hi: 2, x_lo: 2; x = x_hi * 2 + x_lo), y: 8, z: 12, core: 2. Of those that a mesh axis runs over, the one named last changes fastest.
Arguments:
- vectors: bfloat16 [16, 98304], P(None, ('diag', 'off')), may hold values from -6 to 6
- tiles: bfloat16 [32, 24, 32, 128, 128], P('diag', 'off'), may hold values from -0.0625 to 0.0625
- row_index: int32 [32, 24, 32], P('diag', 'off'), may hold values from 0 to 23
- col_index: int32 [32, 24, 32], P('diag', 'off'), may hold values from 0 to 23
- counts: int32 [32, 24], P('diag', 'off'), may hold values from 8 to 32, as said below
Outputs:
- applied: float32 [16, 98304], P(None, ('diag', 'off'))
The draws below stay inside these ranges and needn't reach their ends.
Inputs may be any that keep to these rules, and one draw needn't show every extreme that they name: `counts`: each cell has 8 to 32 live slots, at the front; some cell has exactly 32.
All inputs are finite; a program needn't handle non-finite values.
Results may differ from the reference program's by a relative error of at most 0.0003.
Values may be sent and summed in bfloat16 or wider, within the bound.
A program may use at most 32 MiB of HBM per device.

```python
import jax
import jax.numpy as jnp
from jax import lax

NV = 16
TB = 128
TPG = 24
PAD = 32
NBASIS = 98304
N_DIAG = 32
N_OFF = 24


def draw_counts(key, part):
    key = jax.random.fold_in(key, 7)
    first, second = jax.random.split(key)
    values = jax.random.randint(first, (N_DIAG * N_OFF,), PAD // 4, PAD + 1)
    chosen = jax.random.randint(second, (), 0, N_DIAG * N_OFF)
    values = jnp.where(jnp.arange(N_DIAG * N_OFF) == chosen, PAD, values)
    return values.reshape(N_DIAG, N_OFF).astype(jnp.int32)


def plant(array, rng, smallest, high):
    longest = array.shape.index(max(array.shape))
    spots = []
    for shift in (0, 1):
        where = [jax.random.randint(jax.random.fold_in(rng, axis), (), 0, length) for axis, length in enumerate(array.shape)]
        where[longest] = (where[longest] + shift) % array.shape[longest]
        spots.append(tuple(where))
    return array.at[spots[0]].set(smallest).at[spots[1]].set(high)


def level_of(rng, shape, shards, smallest, largest):
    level = 1.0
    for position, shards_of in shards:
        heights = jax.random.uniform(jax.random.fold_in(jax.random.fold_in(rng, 6), position), (shards_of,), jnp.float32, smallest / len(shards), largest / len(shards))
        level = level * jnp.repeat(jnp.exp(heights), shape[position] // shards_of).reshape((-1,) + (1,) * (len(shape) - 1 - position))
    return level


def scatter_about(stream_key, extent, scale, reach, shards=(), kind=jnp.bfloat16):
    factor_of = level_of(stream_key, extent, shards, -0.22, 0.18) if shards else 1.0
    array = jax.random.normal(stream_key, extent, jnp.float32) * scale * factor_of
    return jnp.minimum(jnp.maximum(array, -reach), reach).astype(kind)


def setup_inputs(seed: int = 0) -> dict:
    arg_keys = jax.random.split(jax.random.key(seed), 6)
    return {
        "vectors": scatter_about(arg_keys[0], (NV, NBASIS), 1.0, 6.0, ((1, 768),)),
        "tiles": scatter_about(arg_keys[1], (N_DIAG, N_OFF, PAD, TB, TB), (2 * TB * PAD * N_OFF // TPG) ** -0.5, 0.0625, ((0, 32), (1, 24))),
        "row_index": plant(jax.random.randint(arg_keys[2], (N_DIAG, N_OFF, PAD), 0, TPG), jax.random.fold_in(arg_keys[2], 1), 0, TPG - 1).astype(jnp.int32),
        "col_index": plant(jax.random.randint(arg_keys[3], (N_DIAG, N_OFF, PAD), 0, TPG), jax.random.fold_in(arg_keys[3], 1), 0, TPG - 1).astype(jnp.int32),
        "counts": draw_counts(jax.random.fold_in(arg_keys[5], 71), 0),
    }


def column_shift(offset, groups, offsets):
    spread = (offset * groups + offsets - 1) // offsets
    return jnp.where(offset == offsets - 1, groups - 1, spread).astype(jnp.int32)


def cell_parts(row_block, col_block, batch, rows, cols, live):
    blocks = row_block.shape[1]
    picked_col = jnp.take(col_block, cols, axis=1).astype(jnp.float32)
    picked_row = jnp.take(row_block, rows, axis=1).astype(jnp.float32)
    wide = batch.astype(jnp.float32)
    forward = jnp.einsum('vpb,pab->vpa', picked_col, wide, precision=lax.Precision.HIGHEST)
    backward = jnp.einsum('vpa,pab->vpb', picked_row, wide, precision=lax.Precision.HIGHEST)
    valid = (jnp.arange(rows.shape[0], dtype=jnp.int32) < live).astype(jnp.float32)
    rows_hot = (rows[:, None] == jnp.arange(blocks, dtype=jnp.int32)[None, :]).astype(jnp.float32) * valid[:, None]
    cols_hot = (cols[:, None] == jnp.arange(blocks, dtype=jnp.int32)[None, :]).astype(jnp.float32) * valid[:, None]
    row_part = jnp.einsum('pt,vpa->vta', rows_hot, forward, precision=lax.Precision.HIGHEST)
    col_part = jnp.einsum('pt,vpb->vtb', cols_hot, backward, precision=lax.Precision.HIGHEST)
    return row_part, col_part


def reference(vectors, tiles, row_index, col_index, counts):
    grouped = vectors.reshape(NV, N_DIAG, TPG, TB)

    def visit(total, cell):
        first = cell // N_OFF
        offset = cell % N_OFF
        other = (first + column_shift(offset, N_DIAG, N_OFF)) % N_DIAG
        row_block = grouped[:, first]
        col_block = grouped[:, other]
        row_part, col_part = cell_parts(row_block, col_block, tiles[first, offset], row_index[first, offset], col_index[first, offset], counts[first, offset])
        total = total.at[:, first].add(row_part)
        total = total.at[:, other].add(col_part)
        return total, None

    start = jnp.zeros((NV, N_DIAG, TPG, TB), jnp.float32)
    total, _ = lax.scan(visit, start, jnp.arange(N_DIAG * N_OFF, dtype=jnp.int32))
    return total.reshape(NV, N_DIAG * TPG * TB)
```

```python
import functools

import jax
import jax.numpy as jnp
from jax import lax
from jax.experimental import pallas as pl
from jax.experimental.pallas import tpu as pltpu
from jax.sharding import PartitionSpec as P

MESH = pl.DeviceIdType.MESH
GROUPS = 32
OFFS = 24
RING = 12
SLOTS = 32


def shift(k):
    return lax.div(k * GROUPS + (OFFS - 1), OFFS)


def peer_steps():
    steps = [(f, d) for f in (0, 1) for d in range(RING)]
    hops = lambda s: 2 * s[0] + min(s[1], RING - s[1])
    return sorted(steps, key=lambda s: (-hops(s), s[1] > RING // 2, s))


STEPS = peer_steps()
AWAY = STEPS[:-1]
N_AWAY = len(AWAY)


def kernel(
    vec, tiles_hbm, row_s, col_s, cnt_s, out,
    tiles, tiles_t, rowv, colv, acc, row_out, col_out, row_in, col_in,
    chain, last,
    tile_sem, send_sem, recv_sem,
):
    i = lax.axis_index("diag")
    k = lax.axis_index("off")
    xh = lax.div(k, RING)
    z = lax.rem(k, RING)
    j = lax.rem(i + shift(k), GROUPS)
    away = k != 0

    def member(step):
        flip, dz = step
        h = 1 - xh if flip else xh
        return h * RING + lax.rem(z + dz, RING)

    def user(t):
        return lax.rem(i - shift(t) + GROUPS, GROUPS)

    barrier = pltpu.get_barrier_semaphore()

    def greet(d, o):
        pl.semaphore_signal(barrier, inc=1, device_id=(d, o), device_id_type=MESH)

    for step in AWAY:
        t = member(step)
        greet(j, t)
        greet(i, t)

    @pl.when(away)
    def _():
        greet(j, k)

    load = pltpu.make_async_copy(tiles_hbm.at[0, 0], tiles, tile_sem)
    load.start()

    rowv[k] = vec[...]

    @pl.when(jnp.logical_not(away))
    def _():
        colv[k] = vec[...]

    acc[SLOTS] = jnp.zeros(acc.shape[1:], jnp.float32)

    pl.semaphore_wait(barrier, 2 * N_AWAY + jnp.where(away, 1, 0))

    def send(src, dst, d, o, sem):
        pltpu.make_async_remote_copy(
            src_ref=src, dst_ref=dst, send_sem=send_sem.at[sem], recv_sem=recv_sem.at[sem],
            device_id=(d, o), device_id_type=MESH,
        ).start()

    def wait(ref, n, sem):
        part = ref.at[pl.ds(0, n)]
        pltpu.make_async_copy(part, part, sem).wait()

    for step in AWAY:
        t = member(step)
        send(vec, colv.at[k], user(t), t, 1)
        send(vec, rowv.at[k], i, t, 0)

    @pl.when(away)
    def _():
        send(vec, colv.at[k], user(k), k, 2)

    live = cnt_s[0, 0]
    rows = [row_s[0, 0, q] for q in range(SLOTS)]
    cols = [col_s[0, 0, q] for q in range(SLOTS)]

    def link(p, _):
        r = row_s[0, 0, p]
        c = col_s[0, 0, p]
        before_r = before_c = jnp.int32(SLOTS)
        for q in range(SLOTS):
            earlier = q < p
            before_r = jnp.where(jnp.logical_and(rows[q] == r, earlier), q, before_r)
            before_c = jnp.where(jnp.logical_and(cols[q] == c, earlier), q, before_c)
        chain[p] = before_r
        chain[SLOTS + p] = before_c
        return 0

    lax.fori_loop(0, SLOTS, link, 0)

    def ends(t, _):
        end_r = end_c = jnp.int32(SLOTS)
        for q in range(SLOTS):
            alive = q < live
            end_r = jnp.where(jnp.logical_and(rows[q] == t, alive), q, end_r)
            end_c = jnp.where(jnp.logical_and(cols[q] == t, alive), q, end_c)
        last[t] = end_r
        last[OFFS + t] = end_c
        return 0

    lax.fori_loop(0, OFFS, ends, 0)

    load.wait()

    def flip(p, _):
        tiles_t[p] = tiles[p].T
        return 0

    lax.fori_loop(0, SLOTS, flip, 0)

    def multiply(picked, idx, mats, base):
        def some(block, _):
            for u in range(8):
                p = block * 8 + u
                x = picked[idx[0, 0, p]]
                y = jnp.dot(x, mats[p], preferred_element_type=jnp.float32)
                acc[p] = acc[chain[base + p]] + y
            return 0

        lax.fori_loop(0, SLOTS // 8, some, 0)

    def settle(part, base):
        for t in range(OFFS):
            part[t] = acc[last[base + t]]

    wait(rowv, N_AWAY, recv_sem.at[0])
    multiply(rowv, row_s, tiles, SLOTS)
    settle(col_out, OFFS)

    wait(colv, N_AWAY, recv_sem.at[1])

    @pl.when(away)
    def _():
        wait(colv, 1, recv_sem.at[2])

    for step in AWAY:
        t = member(step)
        send(col_out.at[t], col_in.at[k], j, t, 4)

    @pl.when(away)
    def _():
        send(col_out.at[k], col_in.at[k], j, k, 5)

    multiply(colv, col_s, tiles_t, 0)
    settle(row_out, 0)
    for step in AWAY:
        t = member(step)
        send(row_out.at[t], row_in.at[k], i, t, 3)
    row_in[k] = row_out[k]

    @pl.when(jnp.logical_not(away))
    def _():
        col_in[k] = col_out[k]

    def total(ref):
        s = ref[0]
        for t in range(1, OFFS):
            s = s + ref[t]
        return s

    wait(col_in, N_AWAY, recv_sem.at[4])

    @pl.when(away)
    def _():
        wait(col_in, 1, recv_sem.at[5])

    cols_sum = total(col_in)
    wait(row_in, N_AWAY, recv_sem.at[3])
    out[...] = cols_sum + total(row_in)

    for sem, ref in ((0, rowv), (1, colv), (3, row_out), (4, col_out)):
        wait(ref, N_AWAY, send_sem.at[sem])

    @pl.when(away)
    def _():
        wait(colv, 1, send_sem.at[2])
        wait(col_out, 1, send_sem.at[5])


def body(vectors, tiles, row_index, col_index, counts):
    nvec, piece = vectors.shape
    smem = pl.BlockSpec(memory_space=pltpu.SMEM)
    vmem = pl.BlockSpec(memory_space=pltpu.VMEM)
    block = (nvec, piece)
    return pl.pallas_call(
        kernel,
        out_shape=jax.ShapeDtypeStruct(block, jnp.float32),
        in_specs=[vmem, pl.BlockSpec(memory_space=pl.ANY), smem, smem, smem],
        out_specs=vmem,
        scratch_shapes=[
            pltpu.VMEM(tiles.shape[2:], tiles.dtype),
            pltpu.VMEM(tiles.shape[2:], tiles.dtype),
            pltpu.VMEM((OFFS,) + block, vectors.dtype),
            pltpu.VMEM((OFFS,) + block, vectors.dtype),
            pltpu.VMEM((SLOTS + 1,) + block, jnp.float32),
            pltpu.VMEM((OFFS,) + block, jnp.float32),
            pltpu.VMEM((OFFS,) + block, jnp.float32),
            pltpu.VMEM((OFFS,) + block, jnp.float32),
            pltpu.VMEM((OFFS,) + block, jnp.float32),
            pltpu.SMEM((2 * SLOTS,), jnp.int32),
            pltpu.SMEM((2 * OFFS,), jnp.int32),
            pltpu.SemaphoreType.DMA,
            pltpu.SemaphoreType.DMA((6,)),
            pltpu.SemaphoreType.DMA((6,)),
        ],
        compiler_params=pltpu.CompilerParams(
            collective_id=0, has_side_effects=True, vmem_limit_bytes=24 * 1024 * 1024
        ),
        cost_estimate=pl.CostEstimate(flops=4 * SLOTS * nvec * piece * piece, bytes_accessed=2 * SLOTS * piece * piece, transcendentals=0),
    )(vectors, tiles, row_index, col_index, counts)


def solution(mesh):
    return jax.shard_map(
        body,
        mesh=mesh,
        in_specs=(
            P(None, ("diag", "off")),
            P("diag", "off", None, None, None),
            P("diag", "off", None),
            P("diag", "off", None),
            P("diag", "off"),
        ),
        out_specs=P(None, ("diag", "off")),
        check_vma=False,
    )
```

```python
import jax
import jax.numpy as jnp
from jax import lax
from jax.experimental import pallas as pl
from jax.experimental.pallas import tpu as pltpu
from jax.sharding import PartitionSpec as P

MESH = pl.DeviceIdType.MESH
GROUPS, OFFS, RING, SLOTS = 32, 24, 12, 32
NEAR=7
def shift(k): return lax.div(k * GROUPS + (OFFS - 1), OFFS)
N_AWAY=OFFS-1
UP=[h*RING+z for z in range(RING) for h in (0,1)]
LINE=[6,5,7,4,8,3,9,2,10,1,11]
def slot(d): return 0 if d==0 else (2*d-1 if d<=RING//2 else 2*(RING-d))
def kernel(vec_h, tiles_h, row_h, col_h, cnt_h, out,
    tiles, tiles_t, rowv, colv, acc, row_out, col_out, row_in, col_in,
    row_s, col_s, cnt_s, chain, last, place, in_sem, send_sem, recv_sem, ready):
    i = lax.axis_index("diag"); k = lax.axis_index("off")
    xh = lax.div(k, RING); z = lax.rem(k, RING)
    j = lax.rem(i + shift(k), GROUPS)
    U=8
    base = xh * RING
    xk=(1-xh)*RING+z
    away = k!=0
    def user(t): return lax.rem(i - shift(jnp.int32(t)) + GROUPS, GROUPS)
    def line(dz): return base + lax.rem(z + dz, RING)
    barrier = pltpu.get_barrier_semaphore()
    def greet(d, o): pl.semaphore_signal(barrier, inc=1, device_id=(d, o), device_id_type=MESH)
    for dz in LINE[:5]: greet(i,line(dz))
    greet(j, xk)
    @pl.when(away)
    def _(): greet(j, k)
    for dz in LINE[5:]: greet(i,line(dz))
    greet(i, xk)
    loads = [pltpu.make_async_copy(a, b, in_sem.at[n]) for n, (a, b) in enumerate(((vec_h, rowv.at[base]), (row_h, row_s), (col_h, col_s), (cnt_h, cnt_s), (tiles_h.at[0, 0], tiles)))]
    for l in loads: l.start()
    acc[SLOTS] = jnp.zeros(acc.shape[1:], jnp.float32)
    loads[0].wait()
    def prework1():
        for l in loads[1:4]: l.wait()
        live = cnt_s[0, 0]
        rows = [row_s[0, 0, q] for q in range(SLOTS)]
        cols = [col_s[0, 0, q] for q in range(SLOTS)]
        def where_lies(t):
            h=lax.div(t,RING)
            d=lax.rem(lax.rem(t,RING)-z+RING,RING)
            return h*RING+jnp.where(d==0,0,jnp.where(d<=RING//2,2*d-1,2*(RING-d)))
        def link(p, _):
            r = row_s[0, 0, p]; c = col_s[0, 0, p]
            place[p]=where_lies(r); place[SLOTS+p]=where_lies(c)
            before_r = before_c = jnp.int32(SLOTS)
            for q in range(SLOTS):
                earlier = q < p
                before_r = jnp.where(jnp.logical_and(rows[q] == r, earlier), q, before_r)
                before_c = jnp.where(jnp.logical_and(cols[q] == c, earlier), q, before_c)
            chain[p] = before_r; chain[SLOTS + p] = before_c
            return 0
        lax.fori_loop(0, SLOTS, link, 0)
        def ends(t, _):
            end_r = end_c = jnp.int32(SLOTS)
            for q in range(SLOTS):
                alive = q < live
                end_r = jnp.where(jnp.logical_and(rows[q] == t, alive), q, end_r)
                end_c = jnp.where(jnp.logical_and(cols[q] == t, alive), q, end_c)
            last[t] = end_r; last[OFFS + t] = end_c
            return 0
        lax.fori_loop(0, OFFS, ends, 0)
    def prework2():
        loads[4].wait()
        def flip(p, _):
            tiles_t[p] = tiles[p].T
            return 0
        lax.fori_loop(0, SLOTS, flip, 0)
    pre=(1, 2)
    if pre[0]==0: prework1()
    if pre[1]==0: prework2()
    pl.semaphore_wait(barrier, len(LINE) + 2 + jnp.where(away, 1, 0))
    def send(src, dst, d, o, sem, rsem=None):
        pltpu.make_async_remote_copy(src_ref=src, dst_ref=dst, send_sem=send_sem.at[sem], recv_sem=recv_sem.at[sem if rsem is None else rsem], device_id=(d, o), device_id_type=MESH).start()
    def wait(ref, n, sem):
        part = ref.at[pl.ds(0, n)]
        pltpu.make_async_copy(part, part, sem).wait()
    mine = rowv.at[base]
    for dz in LINE:
        s=slot((RING-dz)%RING)
        send(mine, rowv.at[base+s], i, line(dz), 0 if s<NEAR else 1)
    pl.semaphore_signal(ready, inc=1, device_id=(user(xk), xk), device_id_type=MESH)
    @pl.when(away)
    def _(): pl.semaphore_signal(ready, inc=1, device_id=(user(k), k), device_id_type=MESH)
    if pre[0]==1: prework1()
    if pre[1]==1: prework2()
    def pass_on(first,n,f):
        part=pl.ds(base+first,n)
        send(rowv.at[part], colv.at[part], user(xk), xk, 2+2*f, 2+2*f+xh)
        @pl.when(away)
        def _(): send(rowv.at[part], colv.at[part], user(k), k, 3+2*f, 2+2*f+xh)
        send(rowv.at[part], rowv.at[part], i, xk, 6+f)
    wait(rowv, NEAR-1, recv_sem.at[0])
    pass_on(0,NEAR,0)
    wait(rowv, RING-NEAR, recv_sem.at[1])
    pass_on(NEAR,RING-NEAR,1)
    @pl.when(jnp.logical_not(away))
    def _(): colv[pl.ds(base,RING)] = rowv[pl.ds(base,RING)]
    if pre[0]==2: prework1()
    if pre[1]==2: prework2()
    def multiply(picked, at, mats, base):
        def some(block, _):
            for u in range(U):
                p = block * U + u
                x = picked[place[at+p]]
                y = jnp.dot(x, mats[p], preferred_element_type=jnp.float32)
                acc[p] = acc[chain[base + p]] + y
            return 0
        if U==SLOTS: some(0,0)
        else: lax.fori_loop(0, SLOTS // U, some, 0)
    wait(rowv, NEAR, recv_sem.at[6])
    wait(rowv, RING-NEAR, recv_sem.at[7])
    multiply(rowv, 0, tiles, SLOTS)
    for t in range(OFFS): col_out[t] = acc[last[OFFS + t]]
    pl.semaphore_wait(ready, 1 + jnp.where(away, 1, 0))
    for t in UP:
        def go(t=t): send(col_out.at[t], col_in.at[k], j, t, 8)
        if t==0: pl.when(away)(go)
        else: go()
    def col_wait(sems,x=None):
        @pl.when(away)
        def _():
            wait(colv, NEAR, sems.at[2]); wait(colv, RING-NEAR, sems.at[4])
        wait(colv, NEAR, sems.at[3]); wait(colv, RING-NEAR, sems.at[5])
    col_wait(recv_sem)
    multiply(colv, SLOTS, tiles_t, 0)
    for t in range(OFFS): row_out[t] = acc[last[t]]
    for t in UP:
        @pl.when(k!=t)
        def _(): send(row_out.at[t], row_in.at[k], i, t, 9)
    row_in[k] = row_out[k]
    @pl.when(jnp.logical_not(away))
    def _(): col_in[0] = col_out[0]
    def total(ref, n):
        s = ref[0]
        for t in range(1, n): s = s + ref[t]
        return s
    def wait_col(ref, sem):
        @pl.when(away)
        def _(): wait(ref,OFFS,sem)
        @pl.when(jnp.logical_not(away))
        def _(): wait(ref,OFFS-1,sem)
    wait_col(col_in, recv_sem.at[8])
    cols_sum = total(col_in, OFFS)
    wait(row_in, OFFS-1, recv_sem.at[9])
    out[...] = cols_sum + total(row_in, OFFS)
    wait(rowv, NEAR-1, send_sem.at[0])
    wait(rowv, RING-NEAR, send_sem.at[1])
    wait(rowv, NEAR, send_sem.at[6])
    wait(rowv, RING-NEAR, send_sem.at[7])
    wait(rowv, NEAR, send_sem.at[2]); wait(rowv, RING-NEAR, send_sem.at[4])
    @pl.when(away)
    def _():
        wait(rowv, NEAR, send_sem.at[3]); wait(rowv, RING-NEAR, send_sem.at[5])
    wait_col(col_out, send_sem.at[8])
    wait(row_out, OFFS-1, send_sem.at[9])
def body(vectors, tiles, row_index, col_index, counts):
    nvec, piece = vectors.shape
    block = (nvec, piece)
    hbm = pl.BlockSpec(memory_space=pltpu.MemorySpace.HBM)
    f32=jnp.float32
    return pl.pallas_call(kernel,
        out_shape=pltpu.MemorySpace.VMEM(block, f32),
        in_specs=[hbm] * 5, out_specs=pl.BlockSpec(memory_space=pltpu.VMEM),
        scratch_shapes=[pltpu.VMEM(tiles.shape[2:], tiles.dtype), pltpu.VMEM(tiles.shape[2:], tiles.dtype),
            pltpu.VMEM((OFFS,) + block, vectors.dtype), pltpu.VMEM((OFFS,) + block, vectors.dtype),
            pltpu.VMEM((SLOTS + 1,) + block, f32)] + [pltpu.VMEM((OFFS,) + block, f32)]*4 + [
            pltpu.SMEM((1,1,SLOTS), jnp.int32), pltpu.SMEM((1,1,SLOTS), jnp.int32), pltpu.SMEM((1,1), jnp.int32),
            pltpu.SMEM((2 * SLOTS,), jnp.int32), pltpu.SMEM((2 * OFFS,), jnp.int32), pltpu.SMEM((2 * SLOTS,), jnp.int32),
            pltpu.SemaphoreType.DMA((5,)), pltpu.SemaphoreType.DMA((10,)), pltpu.SemaphoreType.DMA((10,)), pltpu.SemaphoreType.REGULAR],
        compiler_params=pltpu.CompilerParams(collective_id=0, has_side_effects=True, vmem_limit_bytes=60 * 1024 * 1024),
        cost_estimate=pl.CostEstimate(flops=4 * SLOTS * nvec * piece * piece, bytes_accessed=2 * SLOTS * piece * piece, transcendentals=0),
    )(vectors, tiles, row_index, col_index, counts)


def solution(mesh):
    return jax.shard_map(
        body,
        mesh=mesh,
        in_specs=(
            P(None, ("diag", "off")),
            P("diag", "off", None, None, None),
            P("diag", "off", None),
            P("diag", "off", None),
            P("diag", "off"),
        ),
        out_specs=P(None, ("diag", "off")),
        check_vma=False,
    )
```

```python
import jax
import jax.numpy as jnp
from jax import lax
from jax.experimental import pallas as pl
from jax.experimental.pallas import tpu as pltpu
from jax.sharding import PartitionSpec as P

MESH = pl.DeviceIdType.MESH
GROUPS, OFFS, RING, SLOTS = 32, 24, 12, 32
PIECES = ((0, 1), (1, 4), (5, 4), (9, 3))
NP = len(PIECES)
LOWC, LOWR = 3, 4
LINE = [6, 5, 7, 4, 8, 3, 9, 2, 10, 1, 11]
def shift(k): return lax.div(k * GROUPS + (OFFS - 1), OFFS)
def slot(d): return 0 if d == 0 else (2 * d - 1 if d <= RING // 2 else 2 * (RING - d))
def kernel(vec_h, tiles_h, row_h, col_h, cnt_h, out,
    tiles, rowv, colv, acc, row_out, col_out, row_in, col_in, row_x, col_x,
    row_s, col_s, cnt_s, table_v, table, in_sem, send_sem, recv_sem, ready):
    i = lax.axis_index("diag"); k = lax.axis_index("off")
    xh = lax.div(k, RING); z = lax.rem(k, RING)
    j = lax.rem(i + shift(k), GROUPS)
    base = xh * RING
    xk = (1 - xh) * RING + z
    away = k != 0
    def user(t): return lax.rem(i - shift(jnp.int32(t)) + GROUPS, GROUPS)
    def line(dz): return base + lax.rem(z + dz, RING)
    barrier = pltpu.get_barrier_semaphore()
    def greet(d, o): pl.semaphore_signal(barrier, inc=1, device_id=(d, o), device_id_type=MESH)
    for dz in LINE[:5]: greet(i, line(dz))
    greet(j, xk)
    @pl.when(away)
    def _(): greet(j, k)
    for dz in LINE[5:]: greet(i, line(dz))
    greet(i, xk)
    loads = [pltpu.make_async_copy(a, b, in_sem.at[n]) for n, (a, b) in enumerate(((vec_h, rowv.at[base]), (row_h, row_s), (col_h, col_s), (cnt_h, cnt_s), (tiles_h.at[0, 0], tiles)))]
    for l in loads: l.start()
    acc[SLOTS] = jnp.zeros(acc.shape[1:], jnp.float32)
    to_smem = pltpu.make_async_copy(table_v, table, in_sem.at[5])
    def prepare():
        for l in loads[1:4]: l.wait()
        live = cnt_s[0, 0]
        lane = lax.broadcasted_iota(jnp.int32, (1, 128), 1)
        for side, ref in enumerate((row_s, col_s)):
            every = jnp.zeros((1, 128), jnp.int32)
            for q in range(SLOTS): every = jnp.where(lane == q, ref[0, 0, q], every)
            before = end = jnp.full((1, 128), SLOTS, jnp.int32)
            for q in range(SLOTS):
                t = ref[0, 0, q]
                before = jnp.where(jnp.logical_and(every == t, lane > q), q, before)
                end = jnp.where(lane == jnp.where(q < live, t, -1), q, end)
            d = every - jnp.where(every >= RING, RING, 0) - z
            d = jnp.where(d < 0, d + RING, d)
            lies = jnp.where(every >= RING, RING, 0) + jnp.where(d == 0, 0, jnp.where(d <= RING // 2, 2 * d - 1, 2 * (RING - d)))
            table_v[pl.ds(side, 1)] = before
            table_v[pl.ds(2 + side, 1)] = end
            table_v[pl.ds(4 + side, 1)] = lies
        to_smem.start()
    loads[0].wait()
    prepare()
    pl.semaphore_wait(barrier, len(LINE) + 2 + jnp.where(away, 1, 0))
    def send(src, dst, d, o, sem, rsem=None):
        pltpu.make_async_remote_copy(src_ref=src, dst_ref=dst, send_sem=send_sem.at[sem], recv_sem=recv_sem.at[sem if rsem is None else rsem], device_id=(d, o), device_id_type=MESH).start()
    def wait(ref, n, sem):
        part = ref.at[pl.ds(0, n)]
        pltpu.make_async_copy(part, part, sem).wait()
    mine = rowv.at[base]
    S_LINE, S_X, S_C = 2, 2 + NP, 2 + 2 * NP
    def piece_of(s): return [n for n, (a, c) in enumerate(PIECES) if a <= s < a + c][0]
    for dz in LINE:
        s = slot((RING - dz) % RING)
        send(mine, rowv.at[base + s], i, line(dz), S_LINE + piece_of(s))
    pl.semaphore_signal(ready, inc=1, device_id=(user(xk), xk), device_id_type=MESH)
    @pl.when(away)
    def _(): pl.semaphore_signal(ready, inc=1, device_id=(user(k), k), device_id_type=MESH)
    for n, (a, c) in enumerate(PIECES):
        got = c - (1 if a == 0 else 0)
        if got: wait(rowv, got, recv_sem.at[S_LINE + n])
        part = pl.ds(base + a, c)
        send(rowv.at[part], colv.at[part], user(xk), xk, S_C + 2 * n, S_C + 2 * n + xh)
        @pl.when(away)
        def _(): send(rowv.at[part], colv.at[part], user(k), k, S_C + 2 * n + 1, S_C + 2 * n + xh)
        send(rowv.at[part], rowv.at[part], i, xk, S_X + n)
    @pl.when(jnp.logical_not(away))
    def _(): colv[pl.ds(base, RING)] = rowv[pl.ds(base, RING)]
    loads[4].wait()
    to_smem.wait()
    def multiply(picked, side, axis):
        for p in range(SLOTS):
            x = picked[table[4 + side, p]]
            y = lax.dot_general(x, tiles[p], (((1,), (axis,)), ((), ())), preferred_element_type=jnp.float32)
            acc[p] = acc[table[1 - side, p]] + y
    for n, (a, c) in enumerate(PIECES): wait(rowv, c, recv_sem.at[S_X + n])
    multiply(rowv, 0, 0)
    pl.semaphore_wait(ready, 1 + jnp.where(away, 1, 0))
    partner = lax.rem(i + GROUPS // 2, GROUPS)
    mine_at = lambda first: pl.ds(base + first, RING - first)
    other_at = lambda first: pl.ds(RING - base + first, RING - first)
    def direct(part, into, d, low, sem, skip):
        for zt in range(low):
            for h in (0, 1):
                t = h * RING + zt
                def go(t=t): send(part.at[t], into.at[k], d, t, sem)
                if skip(t) is None: go()
                else: pl.when(skip(t))(go)
    def paired(part, got, into, d, low, sem, x_sem, skip):
        wait(got, RING - low, recv_sem.at[x_sem])
        here = mine_at(low)
        part[here] = part[here] + got[pl.ds(0, RING - low)]
        for zt in range(low, RING):
            def go(zt=zt): send(part.at[base + zt], into.at[z], d, base + zt, sem)
            if skip(zt) is None: go()
            else: pl.when(skip(zt))(go)
    col_skip = lambda t: away if t == 0 else None
    X_COL, X_ROW = S_C + 2 * NP, S_C + 2 * NP + 1
    for t in range(OFFS): col_out[t] = acc[table[3, t]]
    direct(col_out, col_in, j, LOWC, 0, col_skip)
    if LOWC < RING: send(col_out.at[other_at(LOWC)], col_x.at[pl.ds(0, RING - LOWC)], partner, xk, X_COL)
    def col_wait(sems, swap=False):
        for n, (a, c) in enumerate(PIECES):
            @pl.when(away)
            def _(): wait(colv, c, sems.at[S_C + 2 * n + (1 if swap else 0)])
            wait(colv, c, sems.at[S_C + 2 * n + (0 if swap else 1)])
    col_wait(recv_sem)
    multiply(colv, 1, 1)
    for t in range(OFFS): row_out[t] = acc[table[2, t]]
    direct(row_out, row_in, i, LOWR, 1, lambda t: k != t)
    if LOWR < RING: send(row_out.at[other_at(LOWR)], row_x.at[pl.ds(0, RING - LOWR)], i, xk, X_ROW)
    if LOWC < RING: paired(col_out, col_x, col_in, j, LOWC, 0, X_COL, col_skip)
    if LOWR < RING: paired(row_out, row_x, row_in, i, LOWR, 1, X_ROW, lambda zt: z != zt)
    row_in[jnp.where(z < LOWR, k, z)] = row_out[k]
    @pl.when(jnp.logical_not(away))
    def _(): col_in[0] = col_out[0]
    def total(ref, n):
        s = ref[0]
        for t in range(1, n): s = s + ref[t]
        return s
    def finish(ref, low, sem, first):
        def some(n, when):
            @pl.when(when)
            def _():
                if first:
                    @pl.when(away)
                    def _(): wait(ref, n, sem)
                    @pl.when(jnp.logical_not(away))
                    def _(): wait(ref, n - 1, sem)
                    out[...] = total(ref, n)
                else:
                    wait(ref, n - 1, sem)
                    out[...] = out[...] + total(ref, n)
        if low > 0: some(OFFS, z < low)
        if low < RING: some(RING, z >= low)
    finish(col_in, LOWC, recv_sem.at[0], True)
    finish(row_in, LOWR, recv_sem.at[1], False)
    n_col = 2 * LOWC + RING - LOWC; n_row = 2 * LOWR + RING - LOWR - 1
    @pl.when(away)
    def _(): wait(col_out, n_col, send_sem.at[0])
    @pl.when(jnp.logical_not(away))
    def _(): wait(col_out, n_col - 1, send_sem.at[0])
    wait(row_out, n_row, send_sem.at[1])
    if LOWC < RING: wait(col_x, RING - LOWC, send_sem.at[X_COL])
    if LOWR < RING: wait(row_x, RING - LOWR, send_sem.at[X_ROW])
    for n, (a, c) in enumerate(PIECES):
        got = c - (1 if a == 0 else 0)
        if got: wait(rowv, got, send_sem.at[S_LINE + n])
        wait(rowv, c, send_sem.at[S_X + n])
    col_wait(send_sem, True)
def body(vectors, tiles, row_index, col_index, counts):
    nvec, piece = vectors.shape
    block = (nvec, piece)
    hbm = pl.BlockSpec(memory_space=pltpu.MemorySpace.HBM)
    f32 = jnp.float32
    n_sems = 4 + 4 * NP
    return pl.pallas_call(kernel,
        out_shape=pltpu.MemorySpace.VMEM(block, f32),
        in_specs=[hbm] * 5, out_specs=pl.BlockSpec(memory_space=pltpu.VMEM),
        scratch_shapes=[pltpu.VMEM(tiles.shape[2:], tiles.dtype),
            pltpu.VMEM((OFFS,) + block, vectors.dtype), pltpu.VMEM((OFFS,) + block, vectors.dtype),
            pltpu.VMEM((SLOTS + 1,) + block, f32)] + [pltpu.VMEM((OFFS,) + block, f32)]*4 + [pltpu.VMEM((RING,) + block, f32)]*2 + [
            pltpu.SMEM((1, 1, SLOTS), jnp.int32), pltpu.SMEM((1, 1, SLOTS), jnp.int32), pltpu.SMEM((1, 1), jnp.int32),
            pltpu.VMEM((8, 128), jnp.int32), pltpu.SMEM((8, 128), jnp.int32),
            pltpu.SemaphoreType.DMA((6,)), pltpu.SemaphoreType.DMA((n_sems,)), pltpu.SemaphoreType.DMA((n_sems,)), pltpu.SemaphoreType.REGULAR],
        compiler_params=pltpu.CompilerParams(collective_id=0, has_side_effects=True, vmem_limit_bytes=60 * 1024 * 1024),
        cost_estimate=pl.CostEstimate(flops=4 * SLOTS * nvec * piece * piece, bytes_accessed=2 * SLOTS * piece * piece, transcendentals=0),
    )(vectors, tiles, row_index, col_index, counts)


def solution(mesh):
    return jax.shard_map(
        body,
        mesh=mesh,
        in_specs=(
            P(None, ("diag", "off")),
            P("diag", "off", None, None, None),
            P("diag", "off", None),
            P("diag", "off", None),
            P("diag", "off"),
        ),
        out_specs=P(None, ("diag", "off")),
        check_vma=False,
    )
```

```python
import jax
import jax.numpy as jnp
from jax import lax
from jax.experimental import pallas as pl
from jax.experimental.pallas import tpu as pltpu
from jax.sharding import PartitionSpec as P

MESH = pl.DeviceIdType.MESH
GROUPS, OFFS, RING, SLOTS = 32, 24, 12, 32
PIECES = ((0, 1), (1, 4), (5, 4), (9, 3))
NP = len(PIECES)
NEAR_UP, NEAR_DOWN = 3, 3
NEAR = [q for q in range(RING) if q < NEAR_UP or q >= RING - NEAR_DOWN]
LOWC, LOWR = 3, 4
LINE = [6, 5, 7, 4, 8, 3, 9, 2, 10, 1, 11]
def shift(k): return lax.div(k * GROUPS + (OFFS - 1), OFFS)
def slot(d): return 0 if d == 0 else (2 * d - 1 if d <= RING // 2 else 2 * (RING - d))
def kernel(vec_h, tiles_h, row_h, col_h, cnt_h, out,
    tiles, rowv, colv, acc, row_out, col_out, row_in, col_in, row_x, col_x,
    row_s, col_s, cnt_s, table_v, table, in_sem, send_sem, recv_sem, ready):
    i = lax.axis_index("diag"); k = lax.axis_index("off")
    xh = lax.div(k, RING); z = lax.rem(k, RING)
    j = lax.rem(i + shift(k), GROUPS)
    base = xh * RING
    xk = (1 - xh) * RING + z
    away = k != 0
    near = jnp.logical_or(z < NEAR_UP, z >= RING - NEAR_DOWN)
    def either(go):
        pl.when(near)(lambda: go(0, 0))
        pl.when(jnp.logical_not(near))(lambda: go(LOWC, LOWR))
    def user(t): return lax.rem(i - shift(jnp.int32(t)) + GROUPS, GROUPS)
    def line(dz): return base + lax.rem(z + dz, RING)
    barrier = pltpu.get_barrier_semaphore()
    def greet(d, o): pl.semaphore_signal(barrier, inc=1, device_id=(d, o), device_id_type=MESH)
    for dz in LINE[:5]: greet(i, line(dz))
    greet(j, xk)
    @pl.when(away)
    def _(): greet(j, k)
    for dz in LINE[5:]: greet(i, line(dz))
    greet(i, xk)
    loads = [pltpu.make_async_copy(a, b, in_sem.at[n]) for n, (a, b) in enumerate(((vec_h, rowv.at[base]), (row_h, row_s), (col_h, col_s), (cnt_h, cnt_s), (tiles_h.at[0, 0], tiles)))]
    for l in loads: l.start()
    acc[SLOTS] = jnp.zeros(acc.shape[1:], jnp.float32)
    to_smem = pltpu.make_async_copy(table_v, table, in_sem.at[5])
    def prepare():
        for l in loads[1:4]: l.wait()
        live = cnt_s[0, 0]
        lane = lax.broadcasted_iota(jnp.int32, (1, 128), 1)
        for side, ref in enumerate((row_s, col_s)):
            every = jnp.zeros((1, 128), jnp.int32)
            for q in range(SLOTS): every = jnp.where(lane == q, ref[0, 0, q], every)
            before = end = jnp.full((1, 128), SLOTS, jnp.int32)
            for q in range(SLOTS):
                t = ref[0, 0, q]
                before = jnp.where(jnp.logical_and(every == t, lane > q), q, before)
                end = jnp.where(lane == jnp.where(q < live, t, -1), q, end)
            d = every - jnp.where(every >= RING, RING, 0) - z
            d = jnp.where(d < 0, d + RING, d)
            lies = jnp.where(every >= RING, RING, 0) + jnp.where(d == 0, 0, jnp.where(d <= RING // 2, 2 * d - 1, 2 * (RING - d)))
            table_v[pl.ds(side, 1)] = before
            table_v[pl.ds(2 + side, 1)] = end
            table_v[pl.ds(4 + side, 1)] = lies
        to_smem.start()
    loads[0].wait()
    prepare()
    pl.semaphore_wait(barrier, len(LINE) + 2 + jnp.where(away, 1, 0))
    def send(src, dst, d, o, sem, rsem=None):
        pltpu.make_async_remote_copy(src_ref=src, dst_ref=dst, send_sem=send_sem.at[sem], recv_sem=recv_sem.at[sem if rsem is None else rsem], device_id=(d, o), device_id_type=MESH).start()
    def wait(ref, n, sem):
        part = ref.at[pl.ds(0, n)]
        pltpu.make_async_copy(part, part, sem).wait()
    mine = rowv.at[base]
    S_LINE, S_X, S_C = 2, 2 + NP, 2 + 2 * NP
    def piece_of(s): return [n for n, (a, c) in enumerate(PIECES) if a <= s < a + c][0]
    for dz in LINE:
        s = slot((RING - dz) % RING)
        send(mine, rowv.at[base + s], i, line(dz), S_LINE + piece_of(s))
    pl.semaphore_signal(ready, inc=1, device_id=(user(xk), xk), device_id_type=MESH)
    @pl.when(away)
    def _(): pl.semaphore_signal(ready, inc=1, device_id=(user(k), k), device_id_type=MESH)
    for n, (a, c) in enumerate(PIECES):
        got = c - (1 if a == 0 else 0)
        if got: wait(rowv, got, recv_sem.at[S_LINE + n])
        part = pl.ds(base + a, c)
        send(rowv.at[part], colv.at[part], user(xk), xk, S_C + 2 * n, S_C + 2 * n + xh)
        @pl.when(away)
        def _(): send(rowv.at[part], colv.at[part], user(k), k, S_C + 2 * n + 1, S_C + 2 * n + xh)
        send(rowv.at[part], rowv.at[part], i, xk, S_X + n)
    @pl.when(jnp.logical_not(away))
    def _(): colv[pl.ds(base, RING)] = rowv[pl.ds(base, RING)]
    loads[4].wait()
    to_smem.wait()
    def multiply(picked, side, axis):
        for p in range(SLOTS):
            x = picked[table[4 + side, p]]
            y = lax.dot_general(x, tiles[p], (((1,), (axis,)), ((), ())), preferred_element_type=jnp.float32)
            acc[p] = acc[table[1 - side, p]] + y
    for n, (a, c) in enumerate(PIECES): wait(rowv, c, recv_sem.at[S_X + n])
    multiply(rowv, 0, 0)
    pl.semaphore_wait(ready, 1 + jnp.where(away, 1, 0))
    partner = lax.rem(i + GROUPS // 2, GROUPS)
    mine_at = lambda first: pl.ds(base + first, RING - first)
    other_at = lambda first: pl.ds(RING - base + first, RING - first)
    def direct(part, into, d, low, sem, skip):
        for zt in range(low):
            for h in (0, 1):
                t = h * RING + zt
                def go(t=t): send(part.at[t], into.at[k], d, t, sem)
                if skip(t) is None: go()
                else: pl.when(skip(t))(go)
    def paired(part, got, into, d, low, sem, x_sem, skip):
        wait(got, RING - low, recv_sem.at[x_sem])
        here = mine_at(low)
        part[here] = part[here] + got[pl.ds(0, RING - low)]
        for zt in range(low, RING):
            def go(zt=zt): send(part.at[base + zt], into.at[z], d, base + zt, sem)
            if skip(zt) is None: go()
            else: pl.when(skip(zt))(go)
    col_skip = lambda t: away if t == 0 else None
    X_COL, X_ROW = S_C + 2 * NP, S_C + 2 * NP + 1
    for t in range(OFFS): col_out[t] = acc[table[3, t]]
    def col_first(low, _):
        direct(col_out, col_in, j, low, 0, col_skip)
        send(col_out.at[other_at(low)], col_x.at[pl.ds(0, RING - low)], partner, xk, X_COL)
    either(col_first)
    def col_wait(sems, swap=False):
        for n, (a, c) in enumerate(PIECES):
            @pl.when(away)
            def _(): wait(colv, c, sems.at[S_C + 2 * n + (1 if swap else 0)])
            wait(colv, c, sems.at[S_C + 2 * n + (0 if swap else 1)])
    col_wait(recv_sem)
    multiply(colv, 1, 1)
    for t in range(OFFS): row_out[t] = acc[table[2, t]]
    def row_first(lowc, low):
        direct(row_out, row_in, i, low, 1, lambda t: k != t)
        send(row_out.at[other_at(low)], row_x.at[pl.ds(0, RING - low)], i, xk, X_ROW)
        paired(col_out, col_x, col_in, j, lowc, 0, X_COL, col_skip)
        paired(row_out, row_x, row_in, i, low, 1, X_ROW, lambda zt: z != zt)
    either(row_first)
    row_in[jnp.where(jnp.logical_and(z < LOWR, jnp.logical_not(near)), k, z)] = row_out[k]
    @pl.when(jnp.logical_not(away))
    def _(): col_in[0] = col_out[0]
    def total(ref, n):
        used = [q for q in range(OFFS) if q < RING or (n > RING and q - RING not in NEAR)]
        s = ref[used[0]]
        for q in used[1:]: s = s + ref[q]
        return s
    def finish(ref, low, sem, first):
        def some(n, when):
            @pl.when(when)
            def _():
                if first:
                    @pl.when(away)
                    def _(): wait(ref, n, sem)
                    @pl.when(jnp.logical_not(away))
                    def _(): wait(ref, n - 1, sem)
                    out[...] = total(ref, n)
                else:
                    wait(ref, n - 1, sem)
                    out[...] = out[...] + total(ref, n)
        if low > 0: some(OFFS - len(NEAR), z < low)
        if low < RING: some(RING, z >= low)
    finish(col_in, LOWC, recv_sem.at[0], True)
    finish(row_in, LOWR, recv_sem.at[1], False)
    def sent(lowc, lowr):
        n_col = lowc + RING
        @pl.when(away)
        def _(): wait(col_out, n_col, send_sem.at[0])
        @pl.when(jnp.logical_not(away))
        def _(): wait(col_out, n_col - 1, send_sem.at[0])
        wait(row_out, lowr + RING - 1, send_sem.at[1])
        wait(col_x, RING - lowc, send_sem.at[X_COL])
        wait(row_x, RING - lowr, send_sem.at[X_ROW])
    either(sent)
    for n, (a, c) in enumerate(PIECES):
        got = c - (1 if a == 0 else 0)
        if got: wait(rowv, got, send_sem.at[S_LINE + n])
        wait(rowv, c, send_sem.at[S_X + n])
    col_wait(send_sem, True)
def body(vectors, tiles, row_index, col_index, counts):
    nvec, piece = vectors.shape
    block = (nvec, piece)
    hbm = pl.BlockSpec(memory_space=pltpu.MemorySpace.HBM)
    f32 = jnp.float32
    n_sems = 4 + 4 * NP
    return pl.pallas_call(kernel,
        out_shape=pltpu.MemorySpace.VMEM(block, f32),
        in_specs=[hbm] * 5, out_specs=pl.BlockSpec(memory_space=pltpu.VMEM),
        scratch_shapes=[pltpu.VMEM(tiles.shape[2:], tiles.dtype),
            pltpu.VMEM((OFFS,) + block, vectors.dtype), pltpu.VMEM((OFFS,) + block, vectors.dtype),
            pltpu.VMEM((SLOTS + 1,) + block, f32)] + [pltpu.VMEM((OFFS,) + block, f32)]*4 + [pltpu.VMEM((RING,) + block, f32)]*2 + [
            pltpu.SMEM((1, 1, SLOTS), jnp.int32), pltpu.SMEM((1, 1, SLOTS), jnp.int32), pltpu.SMEM((1, 1), jnp.int32),
            pltpu.VMEM((8, 128), jnp.int32), pltpu.SMEM((8, 128), jnp.int32),
            pltpu.SemaphoreType.DMA((6,)), pltpu.SemaphoreType.DMA((n_sems,)), pltpu.SemaphoreType.DMA((n_sems,)), pltpu.SemaphoreType.REGULAR],
        compiler_params=pltpu.CompilerParams(collective_id=0, has_side_effects=True, vmem_limit_bytes=60 * 1024 * 1024),
        cost_estimate=pl.CostEstimate(flops=4 * SLOTS * nvec * piece * piece, bytes_accessed=2 * SLOTS * piece * piece, transcendentals=0),
    )(vectors, tiles, row_index, col_index, counts)


def solution(mesh):
    return jax.shard_map(
        body,
        mesh=mesh,
        in_specs=(
            P(None, ("diag", "off")),
            P("diag", "off", None, None, None),
            P("diag", "off", None),
            P("diag", "off", None),
            P("diag", "off"),
        ),
        out_specs=P(None, ("diag", "off")),
        check_vma=False,
    )
```

```python
import jax
import jax.numpy as jnp
from jax import lax
from jax.experimental import pallas as pl
from jax.experimental.pallas import tpu as pltpu
from jax.sharding import PartitionSpec as P

MESH = pl.DeviceIdType.MESH
GROUPS, OFFS, RING, SLOTS = 32, 24, 12, 32
PIECES = ((0, 1), (1, 4), (5, 4), (9, 3))
NP = len(PIECES)
NEAR_UP, NEAR_DOWN = 1, 1
NEAR = [q for q in range(RING) if q < NEAR_UP or q >= RING - NEAR_DOWN]
LOWC, LOWR = 3, 4
LINE = [6, 5, 7, 4, 8, 3, 9, 2, 10, 1, 11]
def shift(k): return lax.div(k * GROUPS + (OFFS - 1), OFFS)
def slot(d): return 0 if d == 0 else (2 * d - 1 if d <= RING // 2 else 2 * (RING - d))
def kernel(vec_h, tiles_h, row_h, col_h, cnt_h, out,
    tiles, rowv, colv, acc, row_out, col_out, row_in, col_in, row_x, col_x,
    row_s, col_s, cnt_s, table_v, table, in_sem, send_sem, recv_sem, ready):
    i = lax.axis_index("diag"); k = lax.axis_index("off")
    xh = lax.div(k, RING); z = lax.rem(k, RING)
    j = lax.rem(i + shift(k), GROUPS)
    base = xh * RING
    xk = (1 - xh) * RING + z
    away = k != 0
    near = jnp.logical_or(z < NEAR_UP, z >= RING - NEAR_DOWN)
    def either(go):
        pl.when(near)(lambda: go(0, 0))
        pl.when(jnp.logical_not(near))(lambda: go(LOWC, LOWR))
    def user(t): return lax.rem(i - shift(jnp.int32(t)) + GROUPS, GROUPS)
    def line(dz): return base + lax.rem(z + dz, RING)
    barrier = pltpu.get_barrier_semaphore()
    def greet(d, o): pl.semaphore_signal(barrier, inc=1, device_id=(d, o), device_id_type=MESH)
    for dz in LINE[:5]: greet(i, line(dz))
    greet(j, xk)
    @pl.when(away)
    def _(): greet(j, k)
    for dz in LINE[5:]: greet(i, line(dz))
    greet(i, xk)
    loads = [pltpu.make_async_copy(a, b, in_sem.at[n]) for n, (a, b) in enumerate(((vec_h, rowv.at[base]), (row_h, row_s), (col_h, col_s), (cnt_h, cnt_s), (tiles_h.at[0, 0], tiles)))]
    for l in loads: l.start()
    acc[SLOTS] = jnp.zeros(acc.shape[1:], jnp.float32)
    to_smem = pltpu.make_async_copy(table_v, table, in_sem.at[5])
    def prepare():
        for l in loads[1:4]: l.wait()
        live = cnt_s[0, 0]
        lane = lax.broadcasted_iota(jnp.int32, (1, 128), 1)
        for side, ref in enumerate((row_s, col_s)):
            every = jnp.zeros((1, 128), jnp.int32)
            for q in range(SLOTS): every = jnp.where(lane == q, ref[0, 0, q], every)
            before = end = jnp.full((1, 128), SLOTS, jnp.int32)
            for q in range(SLOTS):
                t = ref[0, 0, q]
                before = jnp.where(jnp.logical_and(every == t, lane > q), q, before)
                end = jnp.where(lane == jnp.where(q < live, t, -1), q, end)
            d = every - jnp.where(every >= RING, RING, 0) - z
            d = jnp.where(d < 0, d + RING, d)
            lies = jnp.where(every >= RING, RING, 0) + jnp.where(d == 0, 0, jnp.where(d <= RING // 2, 2 * d - 1, 2 * (RING - d)))
            table_v[pl.ds(side, 1)] = before
            table_v[pl.ds(2 + side, 1)] = end
            table_v[pl.ds(4 + side, 1)] = lies
        to_smem.start()
    loads[0].wait()
    prepare()
    pl.semaphore_wait(barrier, len(LINE) + 2 + jnp.where(away, 1, 0))
    def send(src, dst, d, o, sem, rsem=None):
        pltpu.make_async_remote_copy(src_ref=src, dst_ref=dst, send_sem=send_sem.at[sem], recv_sem=recv_sem.at[sem if rsem is None else rsem], device_id=(d, o), device_id_type=MESH).start()
    def wait(ref, n, sem):
        part = ref.at[pl.ds(0, n)]
        pltpu.make_async_copy(part, part, sem).wait()
    mine = rowv.at[base]
    S_LINE, S_X, S_C = 2, 2 + NP, 2 + 2 * NP
    def piece_of(s): return [n for n, (a, c) in enumerate(PIECES) if a <= s < a + c][0]
    for dz in LINE:
        s = slot((RING - dz) % RING)
        send(mine, rowv.at[base + s], i, line(dz), S_LINE + piece_of(s))
    pl.semaphore_signal(ready, inc=1, device_id=(user(xk), xk), device_id_type=MESH)
    @pl.when(away)
    def _(): pl.semaphore_signal(ready, inc=1, device_id=(user(k), k), device_id_type=MESH)
    for n, (a, c) in enumerate(PIECES):
        got = c - (1 if a == 0 else 0)
        if got: wait(rowv, got, recv_sem.at[S_LINE + n])
        part = pl.ds(base + a, c)
        send(rowv.at[part], colv.at[part], user(xk), xk, S_C + 2 * n, S_C + 2 * n + xh)
        @pl.when(away)
        def _(): send(rowv.at[part], colv.at[part], user(k), k, S_C + 2 * n + 1, S_C + 2 * n + xh)
        send(rowv.at[part], rowv.at[part], i, xk, S_X + n)
    @pl.when(jnp.logical_not(away))
    def _(): colv[pl.ds(base, RING)] = rowv[pl.ds(base, RING)]
    loads[4].wait()
    to_smem.wait()
    def multiply(picked, side, axis):
        for p in range(SLOTS):
            x = picked[table[4 + side, p]]
            y = lax.dot_general(x, tiles[p], (((1,), (axis,)), ((), ())), preferred_element_type=jnp.float32)
            acc[p] = acc[table[1 - side, p]] + y
    for n, (a, c) in enumerate(PIECES): wait(rowv, c, recv_sem.at[S_X + n])
    multiply(rowv, 0, 0)
    pl.semaphore_wait(ready, 1 + jnp.where(away, 1, 0))
    partner = lax.rem(i + GROUPS // 2, GROUPS)
    mine_at = lambda first: pl.ds(base + first, RING - first)
    other_at = lambda first: pl.ds(RING - base + first, RING - first)
    def direct(part, into, d, low, sem, skip):
        for zt in range(low):
            for h in (0, 1):
                t = h * RING + zt
                def go(t=t): send(part.at[t], into.at[k], d, t, sem)
                if skip(t) is None: go()
                else: pl.when(skip(t))(go)
    def paired(part, got, into, d, low, sem, x_sem, skip):
        wait(got, RING - low, recv_sem.at[x_sem])
        here = mine_at(low)
        part[here] = part[here] + got[pl.ds(0, RING - low)]
        for zt in range(low, RING):
            def go(zt=zt): send(part.at[base + zt], into.at[z], d, base + zt, sem)
            if skip(zt) is None: go()
            else: pl.when(skip(zt))(go)
    col_skip = lambda t: away if t == 0 else None
    X_COL, X_ROW = S_C + 2 * NP, S_C + 2 * NP + 1
    for t in range(OFFS): col_out[t] = acc[table[3, t]]
    def col_first(low, _):
        direct(col_out, col_in, j, low, 0, col_skip)
        send(col_out.at[other_at(low)], col_x.at[pl.ds(0, RING - low)], partner, xk, X_COL)
    either(col_first)
    def col_wait(sems, swap=False):
        for n, (a, c) in enumerate(PIECES):
            @pl.when(away)
            def _(): wait(colv, c, sems.at[S_C + 2 * n + (1 if swap else 0)])
            wait(colv, c, sems.at[S_C + 2 * n + (0 if swap else 1)])
    col_wait(recv_sem)
    multiply(colv, 1, 1)
    for t in range(OFFS): row_out[t] = acc[table[2, t]]
    def row_first(lowc, low):
        direct(row_out, row_in, i, low, 1, lambda t: k != t)
        send(row_out.at[other_at(low)], row_x.at[pl.ds(0, RING - low)], i, xk, X_ROW)
        paired(col_out, col_x, col_in, j, lowc, 0, X_COL, col_skip)
        paired(row_out, row_x, row_in, i, low, 1, X_ROW, lambda zt: z != zt)
    either(row_first)
    row_in[jnp.where(jnp.logical_and(z < LOWR, jnp.logical_not(near)), k, z)] = row_out[k]
    @pl.when(jnp.logical_not(away))
    def _(): col_in[0] = col_out[0]
    def total(ref, n):
        used = [q for q in range(OFFS) if q < RING or (n > RING and q - RING not in NEAR)]
        s = ref[used[0]]
        for q in used[1:]: s = s + ref[q]
        return s
    def finish(ref, low, sem, first):
        def some(n, when):
            @pl.when(when)
            def _():
                if first:
                    @pl.when(away)
                    def _(): wait(ref, n, sem)
                    @pl.when(jnp.logical_not(away))
                    def _(): wait(ref, n - 1, sem)
                    out[...] = total(ref, n)
                else:
                    wait(ref, n - 1, sem)
                    out[...] = out[...] + total(ref, n)
        if low > 0: some(OFFS - len(NEAR), z < low)
        if low < RING: some(RING, z >= low)
    finish(col_in, LOWC, recv_sem.at[0], True)
    finish(row_in, LOWR, recv_sem.at[1], False)
    def sent(lowc, lowr):
        n_col = lowc + RING
        @pl.when(away)
        def _(): wait(col_out, n_col, send_sem.at[0])
        @pl.when(jnp.logical_not(away))
        def _(): wait(col_out, n_col - 1, send_sem.at[0])
        wait(row_out, lowr + RING - 1, send_sem.at[1])
        wait(col_x, RING - lowc, send_sem.at[X_COL])
        wait(row_x, RING - lowr, send_sem.at[X_ROW])
    either(sent)
    for n, (a, c) in enumerate(PIECES):
        got = c - (1 if a == 0 else 0)
        if got: wait(rowv, got, send_sem.at[S_LINE + n])
        wait(rowv, c, send_sem.at[S_X + n])
    col_wait(send_sem, True)
def body(vectors, tiles, row_index, col_index, counts):
    nvec, piece = vectors.shape
    block = (nvec, piece)
    hbm = pl.BlockSpec(memory_space=pltpu.MemorySpace.HBM)
    f32 = jnp.float32
    n_sems = 4 + 4 * NP
    return pl.pallas_call(kernel,
        out_shape=pltpu.MemorySpace.VMEM(block, f32),
        in_specs=[hbm] * 5, out_specs=pl.BlockSpec(memory_space=pltpu.VMEM),
        scratch_shapes=[pltpu.VMEM(tiles.shape[2:], tiles.dtype),
            pltpu.VMEM((OFFS,) + block, vectors.dtype), pltpu.VMEM((OFFS,) + block, vectors.dtype),
            pltpu.VMEM((SLOTS + 1,) + block, f32)] + [pltpu.VMEM((OFFS,) + block, f32)]*4 + [pltpu.VMEM((RING,) + block, f32)]*2 + [
            pltpu.SMEM((1, 1, SLOTS), jnp.int32), pltpu.SMEM((1, 1, SLOTS), jnp.int32), pltpu.SMEM((1, 1), jnp.int32),
            pltpu.VMEM((8, 128), jnp.int32), pltpu.SMEM((8, 128), jnp.int32),
            pltpu.SemaphoreType.DMA((6,)), pltpu.SemaphoreType.DMA((n_sems,)), pltpu.SemaphoreType.DMA((n_sems,)), pltpu.SemaphoreType.REGULAR],
        compiler_params=pltpu.CompilerParams(collective_id=0, has_side_effects=True, vmem_limit_bytes=60 * 1024 * 1024),
        cost_estimate=pl.CostEstimate(flops=4 * SLOTS * nvec * piece * piece, bytes_accessed=2 * SLOTS * piece * piece, transcendentals=0),
    )(vectors, tiles, row_index, col_index, counts)


def solution(mesh):
    return jax.shard_map(
        body,
        mesh=mesh,
        in_specs=(
            P(None, ("diag", "off")),
            P("diag", "off", None, None, None),
            P("diag", "off", None),
            P("diag", "off", None),
            P("diag", "off"),
        ),
        out_specs=P(None, ("diag", "off")),
        check_vma=False,
    )
```
